32 devices in a mesh: groups: 2 (over y), col: 4 (over x, core), row: 4 (over z).
Axes of the slice: x: 2, y: 2, z: 4, core: 2. Of those that a mesh axis runs over, the one named last changes fastest.
Arguments:
- features: bfloat16 [128, 128, 256], P(('groups', 'row'), 'col'), parts along dimension 0, may hold values from -6 to 6
- tissue: int32 [128, 128], P(('groups', 'row'), 'col'), parts along dimension 0, may hold values from 0 to 1, as said below
- conv_first: bfloat16 [3, 3, 256, 256], replicated, may hold values from -0.1875 to 0.1875
- bias_first: float32 [256], replicated, may hold values from -3 to 3
- conv_second: bfloat16 [3, 3, 256, 256], replicated, may hold values from -0.1875 to 0.1875
- bias_second: float32 [256], replicated, may hold values from -3 to 3
- key_weight: bfloat16 [256, 1280], replicated, may hold values from -0.375 to 0.375
- value_weight: bfloat16 [256, 1280], replicated, may hold values from -0.375 to 0.375
- latent_queries: bfloat16 [512, 1280], P(('col', 'row')), may hold values from -70 to 70
- out_weight: bfloat16 [1280, 1280], P(None, 'col'), may hold values from -0.15625 to 0.15625
Outputs:
- encoded: bfloat16 [1024, 1280], P(('groups', 'row'), 'col'), parts along dimension 0
The draws below stay inside these ranges and needn't reach their ends.
There are 2 independent parts, one for each index of `groups`. The reference program is written for one: setup_inputs(seed, part) draws one part's arguments, and reference() takes and returns one part's arrays. A program takes and returns all parts, laid end to end along the dimension named above; an argument that names none is the same for every part. Nothing has to cross between parts.
Inputs may be any that keep to these rules, and one draw needn't show every extreme that they name: Every region of 16 x 32 patches of one device holds at least one tissue patch; the share of tissue differs widely from region to region.
All inputs are finite; a program needn't handle non-finite values.
Results may differ from the reference program's by a relative error of at most 0.007.
The reference program's roundings to bfloat16 on the way (of `inputs`, `hidden`, `second`, `key_rows`, `normalized` and `attended`) count: a program that leaves them out, or rounds other values in their place, can miss the bound.
Values may be sent and summed in bfloat16 or wider, within the bound.
A program may use at most 64 MiB of HBM per device.

```python
import math
import jax
import jax.numpy as jnp
from jax import lax

C = 256
E = 1280
Q = 512
PH = 16
PW = 32
GH = 64
GW = 128


def draw_tissue(key, part):
    first_key = jax.random.fold_in(key, 11)
    second_key = jax.random.fold_in(key, 12)
    levels = jax.random.randint(first_key, (GH // PH, GW // PW), 1, 9)
    levels = jnp.repeat(jnp.repeat(levels, PH, axis=0), PW, axis=1)
    cells = jax.random.randint(second_key, (GH, GW), 0, 8)
    chosen = (cells < levels).astype(jnp.int32)
    row_index = lax.broadcasted_iota(jnp.int32, (GH, GW), 0)
    col_index = lax.broadcasted_iota(jnp.int32, (GH, GW), 1)
    corner = jnp.logical_and(row_index % PH == 0, col_index % PW == 0)
    return jnp.where(corner, 1, chosen).astype(jnp.int32)


def draw_latent_queries(key, part):
    base_key = jax.random.fold_in(key, 21)
    values = jnp.clip(2.0 * jax.random.normal(base_key, (Q, E), jnp.float32), -12.0, 12.0)
    return values.astype(jnp.bfloat16)


def block_scale(own_key, dims, split, low, largest):
    level = 1.0
    for position, shards_of in split:
        draws = jax.random.uniform(jax.random.fold_in(jax.random.fold_in(own_key, 6), position), (shards_of,), jnp.float32, low / len(split), largest / len(split))
        level = level * jnp.repeat(jnp.exp(draws), dims[position] // shards_of).reshape((-1,) + (1,) * (len(dims) - 1 - position))
    return level


def centred(key, shape, deviation, reach, cuts=(), held_as=jnp.bfloat16):
    drawn = jax.random.normal(key, shape, jnp.float32) * deviation
    if len(cuts) > 0:
        drawn = block_scale(key, shape, cuts, -0.22, 0.18) * drawn
    return jnp.clip(drawn, min=-reach, max=reach).astype(held_as)


def setup_inputs(seed: int = 0, part: int = 0) -> dict:
    key_of = jax.random.split(jax.random.key(seed), 11)
    part_keys = jax.random.split(jax.random.fold_in(key_of[10], part), 11)
    return {
        "features": centred(part_keys[0], (GH, GW, C), 1.0, 6.0, ((0, 4), (1, 4))),
        "tissue": draw_tissue(jax.random.fold_in(jax.random.fold_in(key_of[10], part), 71), part),
        "conv_first": centred(key_of[2], (3, 3, C, C), (4 * C) ** -0.5, 0.1875),
        "bias_first": centred(key_of[3], (C,), 0.5, 3.0, (), jnp.float32),
        "conv_second": centred(key_of[4], (3, 3, C, C), (4 * C) ** -0.5, 0.1875),
        "bias_second": centred(key_of[5], (C,), 0.5, 3.0, (), jnp.float32),
        "key_weight": centred(key_of[6], (C, E), C ** -0.5, 0.375),
        "value_weight": centred(key_of[7], (C, E), C ** -0.5, 0.375),
        "latent_queries": draw_latent_queries(jax.random.fold_in(key_of[10], 71), part),
        "out_weight": centred(key_of[9], (E, E), E ** -0.5, 0.15625, ((1, 4),)),
    }


def convolve(field_in, weight):
    height, breadth, channels = field_in.shape
    padded = jnp.pad(field_in, ((1, 1), (1, 1), (0, 0)))
    summed = jnp.zeros((height * breadth, weight.shape[3]), jnp.float32)
    for offset_row in range(3):
        for offset_col in range(3):
            window = padded[offset_row:offset_row + height, offset_col:offset_col + breadth]
            summed = summed + jnp.dot(window.reshape(height * breadth, channels), weight[offset_row, offset_col], preferred_element_type=jnp.float32)
    return summed.reshape(height, breadth, weight.shape[3])

def reference(features, tissue, conv_first, bias_first, conv_second, bias_second, key_weight, value_weight, latent_queries, out_weight):
    keep_half = tissue.astype(jnp.bfloat16)
    keep_float = tissue.astype(jnp.float32)[:, :, None]
    inputs = features * keep_half[:, :, None]
    hidden = (jax.nn.gelu(convolve(inputs, conv_first) + bias_first, approximate=False) * keep_float).astype(jnp.bfloat16)
    second = (jax.nn.gelu(convolve(hidden, conv_second) + bias_second, approximate=False) * keep_float).astype(jnp.bfloat16)
    flattened = second.reshape(-1, second.shape[2])
    key_rows = jnp.dot(flattened, key_weight, preferred_element_type=jnp.float32).astype(jnp.bfloat16)
    scale = 1.0 / math.sqrt(latent_queries.shape[1])
    scores = lax.dot_general(latent_queries, key_rows, (((1,), (1,)), ((), ())), preferred_element_type=jnp.float32) * scale
    living = tissue.reshape(-1) > 0
    scores = jnp.where(living[None, :], scores, -1e+30)
    top_score = lax.optimization_barrier(jnp.max(scores, axis=1, keepdims=True))
    weights = jnp.exp(scores - top_score)
    denominator = lax.optimization_barrier(jnp.sum(weights, axis=1, keepdims=True))
    pooled = jnp.dot(weights.astype(jnp.bfloat16), flattened, preferred_element_type=jnp.float32)
    normalized = (pooled / denominator).astype(jnp.bfloat16)
    attended = jnp.dot(normalized, value_weight, preferred_element_type=jnp.float32).astype(jnp.bfloat16)
    return jnp.dot(attended, out_weight, preferred_element_type=jnp.float32).astype(jnp.bfloat16)
```

```python
import functools
import math

import jax
import jax.numpy as jnp
from jax import lax
from jax.experimental import pallas as pl
from jax.experimental.pallas import tpu as pltpu
from jax.sharding import PartitionSpec as P

MESH = pl.DeviceIdType.MESH
LANES = 128
EDGE = 16
DIRS = ((-1, 0), (1, 0), (0, -1), (0, 1), (-1, -1), (-1, 1), (1, -1), (1, 1))


def divisor(total, largest):
    return max(d for d in range(1, largest + 1) if total % d == 0)


def gelu(x):
    return 0.5 * x * (1.0 + lax.erf(x * math.sqrt(0.5)))


def kernel(
    nrow, ncol,
    feat, tis, w1, b1, w2, b2, kw, vw, lq, ow,
    out,
    feat_v, tis_v, w1_v, b1_v, w2_v, b2_v, kw_v, vw_v, ow_v,
    cells, packed, col_out, corner_out, row_in, col_in, corner_in,
    shifted1, hidden, shifted2, second_t, keys, queries,
    pool_out, stat_out, pool_in, stat_in, norm_all,
    load_sem, halo_send, halo_recv, qz_send, qz_recv, qx_send, qx_recv, qp_send, qp_recv,
    pool_send, pool_recv, stat_send, stat_recv, norm_send, norm_recv,
):
    height, breadth, channels = feat.shape
    own, latent = lq.shape
    per_row = own * nrow
    share = channels // ncol
    nx = ncol // 2
    row, col = lax.axis_index("row"), lax.axis_index("col")
    x, core = col // 2, col % 2
    me = row * ncol + col
    reach = breadth + 2 * EDGE
    wide = breadth + EDGE

    loads = [
        pltpu.make_async_copy(src, dst, load_sem.at[i])
        for i, (src, dst) in enumerate(
            [
                (feat, feat_v), (tis, tis_v), (w1, w1_v), (b1, b1_v), (w2, w2_v), (b2, b2_v),
                (kw, kw_v), (vw, vw_v), (ow, ow_v),
                (lq, queries.at[pl.ds(pl.multiple_of((col * nrow + row) * own, own), own)]),
            ]
        )
    ]
    barrier = pltpu.get_barrier_semaphore()
    loads[1].start()
    loads[0].start()
    for step in range(1, nrow * ncol):
        other = lax.rem(me + step, nrow * ncol)
        pl.semaphore_signal(
            barrier, inc=1, device_id={"row": other // ncol, "col": other % ncol},
            device_id_type=MESH,
        )
    for i in (9, 2, 3, 4, 5, 6, 7, 8):
        loads[i].start()

    loads[1].wait()
    mask = jnp.broadcast_to(tis_v[...].astype(jnp.float32)[:, :, None], (height, breadth, LANES))
    loads[0].wait()
    cells[2 : 2 + height, EDGE : EDGE + breadth, channels:] = mask
    packed[:, :, channels:] = mask.astype(jnp.bfloat16)
    for part in range(0, channels, LANES):
        kept = feat_v[:, :, part : part + LANES].astype(jnp.float32) * mask
        cells[2 : 2 + height, EDGE : EDGE + breadth, part : part + LANES] = kept
        packed[:, :, part : part + LANES] = kept.astype(jnp.bfloat16)
    for side, first in enumerate((0, breadth - 2)):
        for ci in range(2):
            col_out[side, ci] = cells[2 : 2 + height, EDGE + first + ci, :].astype(jnp.bfloat16)
    for k, (dr, dc) in enumerate(DIRS[4:]):
        r0 = 2 if dr < 0 else height
        c0 = EDGE if dc < 0 else EDGE + breadth - 2
        rows = [cells[r0 + i, c0 + j : c0 + j + 1, :] for i in range(2) for j in range(2)]
        corner_out[k] = jnp.concatenate(
            rows + [jnp.zeros((EDGE - 4, rows[0].shape[1]), jnp.float32)], axis=0
        ).astype(jnp.bfloat16)

    pl.semaphore_wait(barrier, nrow * ncol - 1)

    def inside(r, c):
        return jnp.logical_and(
            jnp.logical_and(r >= 0, r < nrow), jnp.logical_and(c >= 0, c < ncol)
        )

    def halo_copy(d):
        dr, dc = DIRS[d]
        if d < 2:
            src = packed.at[0:2] if dr < 0 else packed.at[height - 2 : height]
            dst = row_in.at[d]
        elif d < 4:
            src, dst = col_out.at[d - 2], col_in.at[d - 2]
        else:
            src, dst = corner_out.at[d - 4], corner_in.at[d - 4]
        return pltpu.make_async_remote_copy(
            src_ref=src, dst_ref=dst, send_sem=halo_send.at[d], recv_sem=halo_recv.at[d],
            device_id={
                "row": lax.rem(row + dr + nrow, nrow), "col": lax.rem(col + dc + ncol, ncol)
            },
            device_id_type=MESH,
        )

    for d, (dr, dc) in enumerate(DIRS):
        @pl.when(inside(row + dr, col + dc))
        def _():
            halo_copy(d).start()

    def block(c, r):
        return pl.ds(pl.multiple_of((c * nrow + r) * own, own), own)

    def chunk(c):
        return pl.ds(pl.multiple_of(c * per_row, per_row), per_row)

    def z_copy(step, wait=False):
        target = lax.rem(row + step, nrow)
        owner = lax.rem(row - step + nrow, nrow) if wait else row
        return pltpu.make_async_remote_copy(
            src_ref=lq, dst_ref=queries.at[block(col, owner)],
            send_sem=qz_send.at[step], recv_sem=qz_recv.at[step],
            device_id={"row": target}, device_id_type=MESH,
        )

    def x_copy(t, step, wait=False):
        owner = lax.rem(row - step + nrow, nrow)
        source = 2 * lax.rem(x - t + nx, nx) + core if wait else col
        return pltpu.make_async_remote_copy(
            src_ref=lq if step == 0 else queries.at[block(col, owner)],
            dst_ref=queries.at[block(source, owner)],
            send_sem=qx_send.at[t, step], recv_sem=qx_recv.at[t, step],
            device_id={"col": 2 * lax.rem(x + t, nx) + core}, device_id_type=MESH,
        )

    def pair_copy(t, wait=False):
        origin = 2 * lax.rem(x - t + nx, nx) + (1 - core if wait else core)
        return pltpu.make_async_remote_copy(
            src_ref=queries.at[chunk(origin)], dst_ref=queries.at[chunk(origin)],
            send_sem=qp_send.at[t], recv_sem=qp_recv.at[t],
            device_id={"col": 2 * x + 1 - core}, device_id_type=MESH,
        )

    for step in range(1, nrow):
        z_copy(step).start()
    for t in range(1, nx):
        x_copy(t, 0).start()

    for d, (dr, dc) in enumerate(DIRS):
        there = inside(row - dr, col - dc)
        r0 = (2 + height if dr < 0 else 0) if dr else 2
        c0 = (EDGE + breadth if dc < 0 else EDGE - 2) if dc else EDGE

        @pl.when(there)
        def _():
            halo_copy(d).wait_recv()
            if d < 2:
                cells[r0 : r0 + 2, EDGE : EDGE + breadth, :] = row_in[d].astype(jnp.float32)
            elif d < 4:
                for ci in range(2):
                    cells[2 : 2 + height, c0 + ci, :] = col_in[d - 2, ci].astype(jnp.float32)
            else:
                got = corner_in[d - 4].astype(jnp.float32)
                for i in range(2):
                    for j in range(2):
                        cells[r0 + i, c0 + j : c0 + j + 1, :] = got[2 * i + j : 2 * i + j + 1]

        @pl.when(jnp.logical_not(there))
        def _():
            rows = 2 if dr else height
            cols = 2 if dc else breadth
            cells[r0 : r0 + rows, c0 : c0 + cols, :] = jnp.zeros(
                (rows, cols, cells.shape[2]), jnp.float32
            )

    half = EDGE // 2
    for b in range(3):
        shifted1[b] = cells[:, half - 1 + b : half - 1 + b + wide, :channels].astype(jnp.bfloat16)

    loads[2].wait()
    loads[3].wait()
    rows1 = divisor(height + 2, 6)

    @pl.loop(0, (height + 2) // rows1)
    def _(i):
        top = i * rows1
        lhs = jnp.concatenate(
            [
                shifted1[b, pl.ds(top + a, rows1)].reshape(rows1 * wide, channels)
                for a in range(3)
                for b in range(3)
            ],
            axis=1,
        )
        acc = jnp.dot(lhs, w1_v[...], preferred_element_type=jnp.float32)
        acted = gelu(acc + b1_v[...]).reshape(rows1, wide, channels)
        keep = cells[pl.ds(top + 1, rows1), half : half + wide, channels:]
        for part in range(0, channels, LANES):
            hidden[pl.ds(top, rows1), :, part : part + LANES] = (
                acted[:, :, part : part + LANES] * keep
            )

    for step in range(1, nrow):
        z_copy(step, True).wait_recv()
        for t in range(1, nx):
            x_copy(t, step).start()
    loads[9].wait()
    pair_copy(0).start()

    for b in range(3):
        shifted2[b] = hidden[:, half - 1 + b : half - 1 + b + breadth, :].astype(jnp.bfloat16)
    loads[4].wait()
    loads[5].wait()
    loads[6].wait()
    rows2 = divisor(height, 4)
    span = rows2 * breadth
    keep_all = cells[2 : 2 + height, EDGE : EDGE + breadth, channels:].reshape(-1, LANES)

    for i in range(height // rows2):
        top = i * rows2
        lhs = jnp.concatenate(
            [
                shifted2[b, top + a : top + a + rows2].reshape(span, channels)
                for a in range(3)
                for b in range(3)
            ],
            axis=1,
        )
        acc = jnp.dot(lhs, w2_v[...], preferred_element_type=jnp.float32)
        acted = gelu(acc + b2_v[...])
        keep = keep_all[i * span : (i + 1) * span]
        second = jnp.concatenate(
            [acted[:, part : part + LANES] * keep for part in range(0, channels, LANES)], axis=1
        )
        second_t[:, i * span : (i + 1) * span] = second.T.astype(jnp.bfloat16)
        keys[i * span : (i + 1) * span] = jnp.dot(
            second.astype(jnp.bfloat16), kw_v[...], preferred_element_type=jnp.float32
        ).astype(jnp.bfloat16)

    scale = 1.0 / math.sqrt(latent)
    pair_copy(0, True).wait_recv()

    def pool_copy(r, c, source):
        return pltpu.make_async_remote_copy(
            src_ref=pool_out.at[r, pl.ds(pl.multiple_of(c * share, share), share)],
            dst_ref=pool_in.at[source],
            send_sem=pool_send.at[r * ncol + c], recv_sem=pool_recv.at[source],
            device_id={"row": r, "col": c}, device_id_type=MESH,
        )

    def stat_copy(r, c, source):
        return pltpu.make_async_remote_copy(
            src_ref=stat_out.at[r], dst_ref=stat_in.at[source],
            send_sem=stat_send.at[r * ncol + c], recv_sem=stat_recv.at[source],
            device_id={"row": r, "col": c}, device_id_type=MESH,
        )

    for t in range(nx):
        if t:
            for step in range(nrow):
                x_copy(t, step, True).wait_recv()
            pair_copy(t).start()
            pair_copy(t, True).wait_recv()
        kx = lax.rem(x - t + nx, nx)
        got = queries[pl.ds(pl.multiple_of(kx * 2 * per_row, 2 * per_row), 2 * per_row), :]
        scores = (
            lax.dot_general(
                keys[...], got, (((1,), (1,)), ((), ())), preferred_element_type=jnp.float32
            )
            * scale
        )
        living = jnp.concatenate([keep_all] * (2 * per_row // LANES), axis=1) > 0
        scores = jnp.where(living, scores, -1e30)
        top_score = jnp.max(scores, axis=0, keepdims=True)
        weights = jnp.exp(scores - top_score)
        denominator = jnp.sum(weights, axis=0, keepdims=True)
        pooled = jnp.dot(
            second_t[...], weights.astype(jnp.bfloat16), preferred_element_type=jnp.float32
        ).astype(jnp.bfloat16)
        for side in range(2):
            r = 2 * kx + side
            cut = slice(side * per_row, (side + 1) * per_row)
            pool_out[r] = pooled[:, cut]
            stat_out[r, 0:1] = top_score[:, cut]
            stat_out[r, 1:2] = denominator[:, cut]
            for c in range(ncol):
                mine = jnp.logical_and(r == row, c == col)

                @pl.when(jnp.logical_not(mine))
                def _():
                    stat_copy(r, c, me).start()
                    pool_copy(r, c, me).start()

    pool_in[me] = pool_out[row, pl.ds(pl.multiple_of(col * share, share), share), :]
    stat_in[me] = stat_out[row]

    for step in range(1, nrow * ncol):
        source = lax.rem(me + step, nrow * ncol)
        stat_copy(0, 0, source).wait_recv()
    tops = stat_in[:, 0, :]
    best = jnp.max(tops, axis=0, keepdims=True)
    factors = jnp.exp(tops - best)
    denom = jnp.sum(factors * stat_in[:, 1, :], axis=0, keepdims=True)
    for step in range(1, nrow * ncol):
        source = lax.rem(me + step, nrow * ncol)
        pool_copy(0, 0, source).wait_recv()
    total = jnp.zeros((share, per_row), jnp.float32)
    for s in range(nrow * ncol):
        total = total + pool_in[s].astype(jnp.float32) * factors[s : s + 1]
    my_share = pl.ds(pl.multiple_of(col * share, share), share)
    norm_all[my_share, :] = (total / denom).astype(jnp.bfloat16)

    def norm_copy(step, wait=False):
        owner = lax.rem(col - step + ncol, ncol) if wait else col
        place = pl.ds(pl.multiple_of(owner * share, share), share)
        return pltpu.make_async_remote_copy(
            src_ref=norm_all.at[place], dst_ref=norm_all.at[place],
            send_sem=norm_send.at[step], recv_sem=norm_recv.at[step],
            device_id={"col": lax.rem(col + step, ncol)}, device_id_type=MESH,
        )

    for step in range(1, ncol):
        norm_copy(step).start()
    loads[7].wait()
    loads[8].wait()
    for step in range(1, ncol):
        norm_copy(step, True).wait_recv()
    normalized = norm_all[...].astype(jnp.float32).T.astype(jnp.bfloat16)
    attended = jnp.dot(normalized, vw_v[...], preferred_element_type=jnp.float32).astype(
        jnp.bfloat16
    )
    out[...] = jnp.dot(attended, ow_v[...], preferred_element_type=jnp.float32).astype(out.dtype)

    for d, (dr, dc) in enumerate(DIRS):
        @pl.when(inside(row + dr, col + dc))
        def _():
            halo_copy(d).wait_send()
    for step in range(1, nrow):
        z_copy(step).wait_send()
    for t in range(1, nx):
        for step in range(nrow):
            x_copy(t, step).wait_send()
    for t in range(nx):
        pair_copy(t).wait_send()
    for step in range(1, nrow * ncol):
        other = lax.rem(me + step, nrow * ncol)
        stat_copy(other // ncol, other % ncol, me).wait_send()
        pool_copy(other // ncol, other % ncol, me).wait_send()
    for step in range(1, ncol):
        norm_copy(step).wait_send()


def in_one(nrow, ncol, features, tissue, conv_first, bias_first, conv_second, bias_second,
           key_weight, value_weight, latent_queries, out_weight):
    height, breadth, channels = features.shape
    own, latent = latent_queries.shape
    total = own * nrow * ncol
    per_row = total // nrow
    share = channels // ncol
    nx = ncol // 2
    everyone = nrow * ncol
    columns = out_weight.shape[1]
    depth = channels + LANES
    reach = breadth + 2 * EDGE
    wide = breadth + EDGE
    half, full = jnp.bfloat16, jnp.float32
    w1 = conv_first.reshape(-1, conv_first.shape[3])
    w2 = conv_second.reshape(-1, conv_second.shape[3])
    b1 = bias_first.reshape(1, -1)
    b2 = bias_second.reshape(1, -1)
    operands = (features, tissue, w1, b1, w2, b2, key_weight, value_weight, latent_queries,
                out_weight)
    held = [operands[i] for i in (0, 1, 2, 3, 4, 5, 6, 7, 9)]
    dma = pltpu.SemaphoreType.DMA
    return pl.pallas_call(
        functools.partial(kernel, nrow, ncol),
        out_shape=jax.ShapeDtypeStruct((per_row, columns), half),
        in_specs=[pl.BlockSpec(memory_space=pl.ANY)] * len(operands),
        out_specs=pl.BlockSpec(memory_space=pltpu.VMEM),
        scratch_shapes=[pltpu.VMEM(a.shape, a.dtype) for a in held]
        + [
            pltpu.VMEM((height + 4, reach, depth), full),
            pltpu.VMEM((height, breadth, depth), half),
            pltpu.VMEM((2, 2, height, depth), half),
            pltpu.VMEM((4, EDGE, depth), half),
            pltpu.VMEM((2, 2, breadth, depth), half),
            pltpu.VMEM((2, 2, height, depth), half),
            pltpu.VMEM((4, EDGE, depth), half),
            pltpu.VMEM((3, height + 4, wide, channels), half),
            pltpu.VMEM((height + 2, wide, channels), full),
            pltpu.VMEM((3, height + 2, breadth, channels), half),
            pltpu.VMEM((channels, height * breadth), half),
            pltpu.VMEM((height * breadth, latent), half),
            pltpu.VMEM((total, latent), half),
            pltpu.VMEM((nrow, channels, per_row), half),
            pltpu.VMEM((nrow, 8, per_row), full),
            pltpu.VMEM((everyone, share, per_row), half),
            pltpu.VMEM((everyone, 8, per_row), full),
            pltpu.VMEM((channels, per_row), half),
            dma((10,)), dma((8,)), dma((8,)), dma((nrow,)), dma((nrow,)),
            dma((nx, nrow)), dma((nx, nrow)), dma((nx,)), dma((nx,)),
            dma((everyone,)), dma((everyone,)), dma((everyone,)), dma((everyone,)),
            dma((ncol,)), dma((ncol,)),
        ],
        compiler_params=pltpu.CompilerParams(
            collective_id=0, has_side_effects=True, vmem_limit_bytes=50 * 1024 * 1024
        ),
        cost_estimate=pl.CostEstimate(flops=2_500_000_000, bytes_accessed=8_000_000, transcendentals=0),
    )(*operands)


def padded_2(cells, sides, width):
    for axis, dim in sides:
        count = lax.axis_size(axis)
        ends = count - 1
        head = lax.slice_in_dim(cells, 0, width, axis=dim)
        tail = lax.slice_in_dim(cells, cells.shape[dim] - width, cells.shape[dim], axis=dim)
        cells = jnp.concatenate(
            [
                lax.ppermute(tail, axis, [(i, (i + 1) % count) for i in range(ends)]),
                cells,
                lax.ppermute(head, axis, [((i + 1) % count, i) for i in range(ends)]),
            ],
            axis=dim,
        )
    return cells


def convolve_valid(padded, weight, height, breadth):
    channels = padded.shape[2]
    summed = jnp.zeros((height * breadth, weight.shape[3]), jnp.float32)
    for offset_row in range(3):
        for offset_col in range(3):
            window = padded[offset_row : offset_row + height, offset_col : offset_col + breadth]
            summed = summed + jnp.dot(
                window.reshape(height * breadth, channels),
                weight[offset_row, offset_col],
                preferred_element_type=jnp.float32,
            )
    return summed.reshape(height, breadth, weight.shape[3])


def shards(
    features,
    tissue,
    conv_first,
    bias_first,
    conv_second,
    bias_second,
    key_weight,
    value_weight,
    latent_queries,
    out_weight,
):
    height, breadth, channels = features.shape
    keep_half = tissue.astype(jnp.bfloat16)
    keep_float = tissue.astype(jnp.float32)[:, :, None]
    inputs = features * keep_half[:, :, None]
    padded = padded_2(inputs, (("row", 0), ("col", 1)), 1)
    hidden = (
        jax.nn.gelu(
            convolve_valid(padded, conv_first, height, breadth) + bias_first, approximate=False
        )
        * keep_float
    ).astype(jnp.bfloat16)
    beside_all = padded_2(hidden, (("row", 0), ("col", 1)), 1)
    second = (
        jax.nn.gelu(
            convolve_valid(beside_all, conv_second, height, breadth) + bias_second,
            approximate=False,
        )
        * keep_float
    ).astype(jnp.bfloat16)
    flattened = second.reshape(height * breadth, channels)
    key_rows = jnp.dot(flattened, key_weight, preferred_element_type=jnp.float32).astype(
        jnp.bfloat16
    )
    queries = lax.all_gather(latent_queries, ("col", "row"), axis=0, tiled=True)
    latent_size = queries.shape[1]
    scale = 1.0 / math.sqrt(latent_size)
    scores = (
        lax.dot_general(
            queries, key_rows, (((1,), (1,)), ((), ())), preferred_element_type=jnp.float32
        )
        * scale
    )
    living = tissue.reshape(-1) > 0
    scores = jnp.where(living[None, :], scores, -1e30)
    local_top = jnp.max(scores, axis=1)
    top_score = lax.pmax(local_top, ("col", "row"))
    weights = jnp.exp(scores - top_score[:, None])
    denominator = jnp.sum(weights, axis=1)
    pooled = jnp.dot(weights.astype(jnp.bfloat16), flattened, preferred_element_type=jnp.float32)
    pooled_part, denom_part = (
        lax.psum_scatter(pooled, "row", scatter_dimension=0, tiled=True),
        lax.psum_scatter(denominator, "row", scatter_dimension=0, tiled=True),
    )
    pooled_whole, denom_whole = lax.psum((pooled_part, denom_part), "col")
    normalized = (pooled_whole / denom_whole[:, None]).astype(jnp.bfloat16)
    attended = jnp.dot(normalized, value_weight, preferred_element_type=jnp.float32).astype(
        jnp.bfloat16
    )
    return jnp.dot(attended, out_weight, preferred_element_type=jnp.float32).astype(jnp.bfloat16)


def fits(nrow, ncol, arrays):
    height, breadth, channels = arrays[0].shape
    own, latent = arrays[8].shape
    return (
        nrow == ncol
        and ncol % 2 == 0
        and own % 16 == 0
        and (own * ncol) % LANES == 0
        and (channels // ncol) % 16 == 0
        and channels % LANES == 0
        and height % 16 == 0
        and breadth % 16 == 0
        and latent % LANES == 0
    )


def solution(mesh):
    nrow, ncol = mesh.shape["row"], mesh.shape["col"]
    placed = (
        P(("groups", "row"), "col", None),
        P(("groups", "row"), "col"),
        P(),
        P(),
        P(),
        P(),
        P(),
        P(),
        P(("col", "row"), None),
        P(None, "col"),
    )

    def either(*arrays):
        if fits(nrow, ncol, arrays):
            return in_one(nrow, ncol, *arrays)
        return shards(*arrays)

    return jax.shard_map(
        either, mesh=mesh, in_specs=placed, out_specs=P(("groups", "row"), "col"), check_vma=False
    )
```

```python
import functools
import math

import jax
import jax.numpy as jnp
from jax import lax
from jax.experimental import pallas as pl
from jax.experimental.pallas import tpu as pltpu
from jax.sharding import PartitionSpec as P

MESH = pl.DeviceIdType.MESH
LANES = 128
EDGE = 16
DIRS = ((-1, 0), (1, 0), (0, -1), (0, 1), (-1, -1), (-1, 1), (1, -1), (1, 1))


def divisor(total, largest):
    return max(d for d in range(1, largest + 1) if total % d == 0)


def gelu(x):
    return 0.5 * x * (1.0 + lax.erf(x * math.sqrt(0.5)))


def kernel(
    nrow, ncol,
    feat, tis, w1, b1, w2, b2, kw, vw, lq, ow,
    out,
    feat_v, tis_v, w1_v, b1_v, w2_v, b2_v, kw_v, vw_v, ow_v,
    cells, packed, col_out, corner_out, row_in, col_in, corner_in,
    shifted1, hidden, shifted2, second_own, second_in, keep_in, second_t, keys, queries,
    pool_out, stat_out, pool_in, stat_in, norm_all,
    load_sem, halo_send, halo_recv, qz_send, qz_recv, qx_send, qx_recv, pair_send, pair_recv,
    pool_send, pool_recv, stat_send, stat_recv, norm_send, norm_recv,
):
    height, breadth, channels = feat.shape
    own, latent = lq.shape
    per_row = own * nrow
    share = channels // ncol
    nx = ncol // 2
    row, col = lax.axis_index("row"), lax.axis_index("col")
    x, core = col // 2, col % 2
    me = row * ncol + col
    me_chip = row * nx + x
    rows2 = divisor(height, 4)
    span = rows2 * breadth
    spans = height // rows2
    count = height * breadth
    wide = breadth + EDGE

    loads = [
        pltpu.make_async_copy(src, dst, load_sem.at[i])
        for i, (src, dst) in enumerate(
            [
                (feat, feat_v), (tis, tis_v), (w1, w1_v), (b1, b1_v), (w2, w2_v), (b2, b2_v),
                (kw, kw_v), (vw, vw_v), (ow, ow_v),
                (lq, queries.at[pl.ds(pl.multiple_of((col * nrow + row) * own, own), own)]),
            ]
        )
    ]
    barrier = pltpu.get_barrier_semaphore()
    loads[1].start()
    loads[0].start()
    for step in range(1, nrow * ncol):
        other = lax.rem(me + step, nrow * ncol)
        pl.semaphore_signal(
            barrier, inc=1, device_id={"row": other // ncol, "col": other % ncol},
            device_id_type=MESH,
        )
    for i in (9, 2, 3, 4, 5, 6, 7, 8):
        loads[i].start()

    loads[1].wait()
    mask = jnp.broadcast_to(tis_v[...].astype(jnp.float32)[:, :, None], (height, breadth, LANES))
    loads[0].wait()
    cells[2 : 2 + height, EDGE : EDGE + breadth, channels:] = mask
    packed[:, :, channels:] = mask.astype(jnp.bfloat16)
    for part in range(0, channels, LANES):
        kept = feat_v[:, :, part : part + LANES].astype(jnp.float32) * mask
        cells[2 : 2 + height, EDGE : EDGE + breadth, part : part + LANES] = kept
        packed[:, :, part : part + LANES] = kept.astype(jnp.bfloat16)
    for side, first in enumerate((0, breadth - 2)):
        for ci in range(2):
            col_out[side, ci] = cells[2 : 2 + height, EDGE + first + ci, :].astype(jnp.bfloat16)
    for k, (dr, dc) in enumerate(DIRS[4:]):
        r0 = 2 if dr < 0 else height
        c0 = EDGE if dc < 0 else EDGE + breadth - 2
        rows = [cells[r0 + i, c0 + j : c0 + j + 1, :] for i in range(2) for j in range(2)]
        corner_out[k] = jnp.concatenate(
            rows + [jnp.zeros((EDGE - 4, rows[0].shape[1]), jnp.float32)], axis=0
        ).astype(jnp.bfloat16)

    pl.semaphore_wait(barrier, nrow * ncol - 1)

    def inside(r, c):
        return jnp.logical_and(
            jnp.logical_and(r >= 0, r < nrow), jnp.logical_and(c >= 0, c < ncol)
        )

    def halo_copy(d):
        dr, dc = DIRS[d]
        if d < 2:
            src = packed.at[0:2] if dr < 0 else packed.at[height - 2 : height]
            dst = row_in.at[d]
        elif d < 4:
            src, dst = col_out.at[d - 2], col_in.at[d - 2]
        else:
            src, dst = corner_out.at[d - 4], corner_in.at[d - 4]
        return pltpu.make_async_remote_copy(
            src_ref=src, dst_ref=dst, send_sem=halo_send.at[d], recv_sem=halo_recv.at[d],
            device_id={
                "row": lax.rem(row + dr + nrow, nrow), "col": lax.rem(col + dc + ncol, ncol)
            },
            device_id_type=MESH,
        )

    for d, (dr, dc) in enumerate(DIRS):
        @pl.when(inside(row + dr, col + dc))
        def _():
            halo_copy(d).start()

    def block(c, r):
        return pl.ds(pl.multiple_of((c * nrow + r) * own, own), own)

    def chunk(c):
        return pl.ds(pl.multiple_of(c * per_row, per_row), per_row)

    def z_copy(step, wait=False):
        target = lax.rem(row + step, nrow)
        owner = lax.rem(row - step + nrow, nrow) if wait else row
        return pltpu.make_async_remote_copy(
            src_ref=lq, dst_ref=queries.at[block(col, owner)],
            send_sem=qz_send.at[step], recv_sem=qz_recv.at[step],
            device_id={"row": target}, device_id_type=MESH,
        )

    def x_copy(t, step, wait=False):
        owner = lax.rem(row - step + nrow, nrow)
        source = 2 * lax.rem(x - t + nx, nx) + core if wait else col
        return pltpu.make_async_remote_copy(
            src_ref=lq if step == 0 else queries.at[block(col, owner)],
            dst_ref=queries.at[block(source, owner)],
            send_sem=qx_send.at[t, step], recv_sem=qx_recv.at[t, step],
            device_id={"col": 2 * lax.rem(x + t, nx) + core}, device_id_type=MESH,
        )

    def pair_copy(i):
        if i < spans:
            src = second_own.at[i * span : (i + 1) * span]
            dst = second_in.at[i * span : (i + 1) * span]
        else:
            src, dst = packed.at[:, :, channels:], keep_in
        return pltpu.make_async_remote_copy(
            src_ref=src, dst_ref=dst, send_sem=pair_send.at[i], recv_sem=pair_recv.at[i],
            device_id={"col": 2 * x + 1 - core}, device_id_type=MESH,
        )

    pair_copy(spans).start()
    for step in range(1, nrow):
        z_copy(step).start()
    for t in range(1, nx):
        x_copy(t, 0).start()

    for d, (dr, dc) in enumerate(DIRS):
        there = inside(row - dr, col - dc)
        r0 = (2 + height if dr < 0 else 0) if dr else 2
        c0 = (EDGE + breadth if dc < 0 else EDGE - 2) if dc else EDGE

        @pl.when(there)
        def _():
            halo_copy(d).wait_recv()
            if d < 2:
                cells[r0 : r0 + 2, EDGE : EDGE + breadth, :] = row_in[d].astype(jnp.float32)
            elif d < 4:
                for ci in range(2):
                    cells[2 : 2 + height, c0 + ci, :] = col_in[d - 2, ci].astype(jnp.float32)
            else:
                got = corner_in[d - 4].astype(jnp.float32)
                for i in range(2):
                    for j in range(2):
                        cells[r0 + i, c0 + j : c0 + j + 1, :] = got[2 * i + j : 2 * i + j + 1]

        @pl.when(jnp.logical_not(there))
        def _():
            rows = 2 if dr else height
            cols = 2 if dc else breadth
            cells[r0 : r0 + rows, c0 : c0 + cols, :] = jnp.zeros(
                (rows, cols, cells.shape[2]), jnp.float32
            )

    half = EDGE // 2
    for b in range(3):
        shifted1[b] = cells[:, half - 1 + b : half - 1 + b + wide, :channels].astype(jnp.bfloat16)

    loads[2].wait()
    loads[3].wait()
    rows1 = divisor(height + 2, 6)

    @pl.loop(0, (height + 2) // rows1)
    def _(i):
        top = i * rows1
        lhs = jnp.concatenate(
            [
                shifted1[b, pl.ds(top + a, rows1)].reshape(rows1 * wide, channels)
                for a in range(3)
                for b in range(3)
            ],
            axis=1,
        )
        acc = jnp.dot(lhs, w1_v[...], preferred_element_type=jnp.float32)
        acted = gelu(acc + b1_v[...]).reshape(rows1, wide, channels)
        keep = cells[pl.ds(top + 1, rows1), half : half + wide, channels:]
        for part in range(0, channels, LANES):
            hidden[pl.ds(top, rows1), :, part : part + LANES] = (
                acted[:, :, part : part + LANES] * keep
            )

    def hand_on(step):
        z_copy(step, True).wait_recv()
        for t in range(1, nx):
            x_copy(t, step).start()

    for b in range(3):
        shifted2[b] = hidden[:, half - 1 + b : half - 1 + b + breadth, :].astype(jnp.bfloat16)
    loads[4].wait()
    loads[5].wait()
    loads[6].wait()
    keep_all = cells[2 : 2 + height, EDGE : EDGE + breadth, channels:].reshape(-1, LANES)

    for i in range(spans):
        top = i * rows2
        lhs = jnp.concatenate(
            [
                shifted2[b, top + a : top + a + rows2].reshape(span, channels)
                for a in range(3)
                for b in range(3)
            ],
            axis=1,
        )
        acc = jnp.dot(lhs, w2_v[...], preferred_element_type=jnp.float32)
        acted = gelu(acc + b2_v[...])
        keep = keep_all[i * span : (i + 1) * span]
        second = jnp.concatenate(
            [acted[:, part : part + LANES] * keep for part in range(0, channels, LANES)], axis=1
        )
        second_half = second.astype(jnp.bfloat16)
        second_own[i * span : (i + 1) * span] = second_half
        pair_copy(i).start()
        second_t[:, i * span : (i + 1) * span] = second.T.astype(jnp.bfloat16)
        keys[i * span : (i + 1) * span] = jnp.dot(
            second_half, kw_v[...], preferred_element_type=jnp.float32
        ).astype(jnp.bfloat16)
        if i + 1 < nrow:
            hand_on(i + 1)
    for step in range(spans + 1, nrow):
        hand_on(step)

    for i in range(spans):
        pair_copy(i).wait_recv()
        second_half = second_in[i * span : (i + 1) * span]
        place = slice(count + i * span, count + (i + 1) * span)
        second_t[:, place] = second_half.astype(jnp.float32).T.astype(jnp.bfloat16)
        keys[place] = jnp.dot(
            second_half, kw_v[...], preferred_element_type=jnp.float32
        ).astype(jnp.bfloat16)
    pair_copy(spans).wait_recv()
    living = (
        jnp.concatenate(
            [keep_all, keep_in[...].astype(jnp.float32).reshape(-1, LANES)], axis=0
        )
        > 0
    )
    living = jnp.concatenate([living] * (per_row // LANES), axis=1)

    scale = 1.0 / math.sqrt(latent)
    loads[9].wait()

    def pool_copy(r, c, source):
        return pltpu.make_async_remote_copy(
            src_ref=pool_out.at[r, pl.ds(pl.multiple_of(c * share, share), share)],
            dst_ref=pool_in.at[source],
            send_sem=pool_send.at[r * ncol + c], recv_sem=pool_recv.at[source],
            device_id={"row": r, "col": c}, device_id_type=MESH,
        )

    def stat_copy(r, c, source):
        return pltpu.make_async_remote_copy(
            src_ref=stat_out.at[r], dst_ref=stat_in.at[source],
            send_sem=stat_send.at[r * ncol + c], recv_sem=stat_recv.at[source],
            device_id={"row": r, "col": c}, device_id_type=MESH,
        )

    for t in range(nx):
        if t:
            for step in range(nrow):
                x_copy(t, step, True).wait_recv()
        r = 2 * lax.rem(x - t + nx, nx) + core
        got = queries[chunk(r), :]
        scores = (
            lax.dot_general(
                keys[...], got, (((1,), (1,)), ((), ())), preferred_element_type=jnp.float32
            )
            * scale
        )
        scores = jnp.where(living, scores, -1e30)
        top_score = jnp.max(scores, axis=0, keepdims=True)
        weights = jnp.exp(scores - top_score)
        denominator = jnp.sum(weights, axis=0, keepdims=True)
        pooled = jnp.dot(
            second_t[...], weights.astype(jnp.bfloat16), preferred_element_type=jnp.float32
        ).astype(jnp.bfloat16)
        pool_out[r] = pooled
        stat_out[r, 0:1] = top_score
        stat_out[r, 1:2] = denominator
        for c in range(ncol):
            @pl.when(jnp.logical_not(jnp.logical_and(r == row, c == col)))
            def _():
                stat_copy(r, c, me_chip).start()
                pool_copy(r, c, me_chip).start()

    own_part = core == row % 2

    @pl.when(own_part)
    def _():
        pool_in[me_chip] = pool_out[row, pl.ds(pl.multiple_of(col * share, share), share), :]
        stat_in[me_chip] = stat_out[row]

    def from_all(copy):
        for source in range(nrow * nx):
            @pl.when(jnp.logical_not(jnp.logical_and(own_part, source == me_chip)))
            def _():
                copy(0, 0, source).wait_recv()

    from_all(stat_copy)
    tops = stat_in[:, 0, :]
    best = jnp.max(tops, axis=0, keepdims=True)
    factors = jnp.exp(tops - best)
    denom = jnp.sum(factors * stat_in[:, 1, :], axis=0, keepdims=True)
    from_all(pool_copy)
    total = jnp.zeros((share, per_row), jnp.float32)
    for s in range(nrow * nx):
        total = total + pool_in[s].astype(jnp.float32) * factors[s : s + 1]
    my_share = pl.ds(pl.multiple_of(col * share, share), share)
    norm_all[my_share, :] = (total / denom).astype(jnp.bfloat16)

    def norm_copy(step, wait=False):
        owner = lax.rem(col - step + ncol, ncol) if wait else col
        place = pl.ds(pl.multiple_of(owner * share, share), share)
        return pltpu.make_async_remote_copy(
            src_ref=norm_all.at[place], dst_ref=norm_all.at[place],
            send_sem=norm_send.at[step], recv_sem=norm_recv.at[step],
            device_id={"col": lax.rem(col + step, ncol)}, device_id_type=MESH,
        )

    for step in range(1, ncol):
        norm_copy(step).start()
    loads[7].wait()
    loads[8].wait()
    for step in range(1, ncol):
        norm_copy(step, True).wait_recv()
    normalized = norm_all[...].astype(jnp.float32).T.astype(jnp.bfloat16)
    attended = jnp.dot(normalized, vw_v[...], preferred_element_type=jnp.float32).astype(
        jnp.bfloat16
    )
    out[...] = lax.dot_general(
        ow_v[...], attended, (((1,), (1,)), ((), ())), preferred_element_type=jnp.float32
    ).astype(out.dtype)

    for d, (dr, dc) in enumerate(DIRS):
        @pl.when(inside(row + dr, col + dc))
        def _():
            halo_copy(d).wait_send()
    for step in range(1, nrow):
        z_copy(step).wait_send()
    for t in range(1, nx):
        for step in range(nrow):
            x_copy(t, step).wait_send()
    for i in range(spans + 1):
        pair_copy(i).wait_send()
    for t in range(nx):
        r = 2 * lax.rem(x - t + nx, nx) + core
        for c in range(ncol):
            @pl.when(jnp.logical_not(jnp.logical_and(r == row, c == col)))
            def _():
                stat_copy(r, c, me_chip).wait_send()
                pool_copy(r, c, me_chip).wait_send()
    for step in range(1, ncol):
        norm_copy(step).wait_send()


def in_one(nrow, ncol, features, tissue, conv_first, bias_first, conv_second, bias_second,
           key_weight, value_weight, latent_queries, out_weight):
    height, breadth, channels = features.shape
    own, latent = latent_queries.shape
    total = own * nrow * ncol
    per_row = total // nrow
    share = channels // ncol
    nx = ncol // 2
    everyone = nrow * ncol
    sources = nrow * nx
    spans = height // divisor(height, 4) + 1
    columns = out_weight.shape[1]
    depth = channels + LANES
    reach = breadth + 2 * EDGE
    wide = breadth + EDGE
    half, full = jnp.bfloat16, jnp.float32
    w1 = conv_first.reshape(-1, conv_first.shape[3])
    w2 = conv_second.reshape(-1, conv_second.shape[3])
    b1 = bias_first.reshape(1, -1)
    b2 = bias_second.reshape(1, -1)
    operands = (features, tissue, w1, b1, w2, b2, key_weight, value_weight, latent_queries,
                out_weight.T)
    held = [operands[i] for i in (0, 1, 2, 3, 4, 5, 6, 7, 9)]
    dma = pltpu.SemaphoreType.DMA
    return pl.pallas_call(
        functools.partial(kernel, nrow, ncol),
        out_shape=jax.ShapeDtypeStruct((columns, per_row), half),
        in_specs=[pl.BlockSpec(memory_space=pltpu.HBM)] * len(operands),
        out_specs=pl.BlockSpec(memory_space=pltpu.VMEM),
        scratch_shapes=[pltpu.VMEM(a.shape, a.dtype) for a in held]
        + [
            pltpu.VMEM((height + 4, reach, depth), full),
            pltpu.VMEM((height, breadth, depth), half),
            pltpu.VMEM((2, 2, height, depth), half),
            pltpu.VMEM((4, EDGE, depth), half),
            pltpu.VMEM((2, 2, breadth, depth), half),
            pltpu.VMEM((2, 2, height, depth), half),
            pltpu.VMEM((4, EDGE, depth), half),
            pltpu.VMEM((3, height + 4, wide, channels), half),
            pltpu.VMEM((height + 2, wide, channels), full),
            pltpu.VMEM((3, height + 2, breadth, channels), half),
            pltpu.VMEM((height * breadth, channels), half),
            pltpu.VMEM((height * breadth, channels), half),
            pltpu.VMEM((height, breadth, LANES), half),
            pltpu.VMEM((channels, 2 * height * breadth), half),
            pltpu.VMEM((2 * height * breadth, latent), half),
            pltpu.VMEM((total, latent), half),
            pltpu.VMEM((nrow, channels, per_row), half),
            pltpu.VMEM((nrow, 8, per_row), full),
            pltpu.VMEM((sources, share, per_row), half),
            pltpu.VMEM((sources, 8, per_row), full),
            pltpu.VMEM((channels, per_row), half),
            dma((10,)), dma((8,)), dma((8,)), dma((nrow,)), dma((nrow,)),
            dma((nx, nrow)), dma((nx, nrow)), dma((spans,)), dma((spans,)),
            dma((everyone,)), dma((sources,)), dma((everyone,)), dma((sources,)),
            dma((ncol,)), dma((ncol,)),
        ],
        compiler_params=pltpu.CompilerParams(
            collective_id=0, has_side_effects=True, vmem_limit_bytes=63 * 1024 * 1024
        ),
        cost_estimate=pl.CostEstimate(flops=2_500_000_000, bytes_accessed=8_000_000, transcendentals=0),
    )(*operands).T


def padded_2(cells, sides, width):
    for axis, dim in sides:
        count = lax.axis_size(axis)
        ends = count - 1
        head = lax.slice_in_dim(cells, 0, width, axis=dim)
        tail = lax.slice_in_dim(cells, cells.shape[dim] - width, cells.shape[dim], axis=dim)
        cells = jnp.concatenate(
            [
                lax.ppermute(tail, axis, [(i, (i + 1) % count) for i in range(ends)]),
                cells,
                lax.ppermute(head, axis, [((i + 1) % count, i) for i in range(ends)]),
            ],
            axis=dim,
        )
    return cells


def convolve_valid(padded, weight, height, breadth):
    channels = padded.shape[2]
    summed = jnp.zeros((height * breadth, weight.shape[3]), jnp.float32)
    for offset_row in range(3):
        for offset_col in range(3):
            window = padded[offset_row : offset_row + height, offset_col : offset_col + breadth]
            summed = summed + jnp.dot(
                window.reshape(height * breadth, channels),
                weight[offset_row, offset_col],
                preferred_element_type=jnp.float32,
            )
    return summed.reshape(height, breadth, weight.shape[3])


def shards(
    features,
    tissue,
    conv_first,
    bias_first,
    conv_second,
    bias_second,
    key_weight,
    value_weight,
    latent_queries,
    out_weight,
):
    height, breadth, channels = features.shape
    keep_half = tissue.astype(jnp.bfloat16)
    keep_float = tissue.astype(jnp.float32)[:, :, None]
    inputs = features * keep_half[:, :, None]
    padded = padded_2(inputs, (("row", 0), ("col", 1)), 1)
    hidden = (
        jax.nn.gelu(
            convolve_valid(padded, conv_first, height, breadth) + bias_first, approximate=False
        )
        * keep_float
    ).astype(jnp.bfloat16)
    beside_all = padded_2(hidden, (("row", 0), ("col", 1)), 1)
    second = (
        jax.nn.gelu(
            convolve_valid(beside_all, conv_second, height, breadth) + bias_second,
            approximate=False,
        )
        * keep_float
    ).astype(jnp.bfloat16)
    flattened = second.reshape(height * breadth, channels)
    key_rows = jnp.dot(flattened, key_weight, preferred_element_type=jnp.float32).astype(
        jnp.bfloat16
    )
    queries = lax.all_gather(latent_queries, ("col", "row"), axis=0, tiled=True)
    latent_size = queries.shape[1]
    scale = 1.0 / math.sqrt(latent_size)
    scores = (
        lax.dot_general(
            queries, key_rows, (((1,), (1,)), ((), ())), preferred_element_type=jnp.float32
        )
        * scale
    )
    living = tissue.reshape(-1) > 0
    scores = jnp.where(living[None, :], scores, -1e30)
    local_top = jnp.max(scores, axis=1)
    top_score = lax.pmax(local_top, ("col", "row"))
    weights = jnp.exp(scores - top_score[:, None])
    denominator = jnp.sum(weights, axis=1)
    pooled = jnp.dot(weights.astype(jnp.bfloat16), flattened, preferred_element_type=jnp.float32)
    pooled_part, denom_part = (
        lax.psum_scatter(pooled, "row", scatter_dimension=0, tiled=True),
        lax.psum_scatter(denominator, "row", scatter_dimension=0, tiled=True),
    )
    pooled_whole, denom_whole = lax.psum((pooled_part, denom_part), "col")
    normalized = (pooled_whole / denom_whole[:, None]).astype(jnp.bfloat16)
    attended = jnp.dot(normalized, value_weight, preferred_element_type=jnp.float32).astype(
        jnp.bfloat16
    )
    return jnp.dot(attended, out_weight, preferred_element_type=jnp.float32).astype(jnp.bfloat16)


def fits(nrow, ncol, arrays):
    height, breadth, channels = arrays[0].shape
    own, latent = arrays[8].shape
    return (
        nrow == ncol
        and ncol % 2 == 0
        and own % 16 == 0
        and (own * ncol) % LANES == 0
        and (channels // ncol) % 16 == 0
        and channels % LANES == 0
        and height % 16 == 0
        and breadth % 16 == 0
        and latent % LANES == 0
    )


def solution(mesh):
    nrow, ncol = mesh.shape["row"], mesh.shape["col"]
    placed = (
        P(("groups", "row"), "col", None),
        P(("groups", "row"), "col"),
        P(),
        P(),
        P(),
        P(),
        P(),
        P(),
        P(("col", "row"), None),
        P(None, "col"),
    )

    def either(*arrays):
        if fits(nrow, ncol, arrays):
            return in_one(nrow, ncol, *arrays)
        return shards(*arrays)

    return jax.shard_map(
        either, mesh=mesh, in_specs=placed, out_specs=P(("groups", "row"), "col"), check_vma=False
    )
```
